32 devices in a mesh: groups: 1, px: 32 (over z, y, x, core).
Axes of the slice: x: 2, y: 2, z: 4, core: 2. Of those that a mesh axis runs over, the one named last changes fastest.
Arguments:
- fields: bfloat16 [9, 64, 256, 256], P('groups', 'px'), may hold values from -6 to 6
- target: bfloat16 [6, 64, 256, 256], P('groups', 'px'), may hold values from -34 to 34
- lift_weight: bfloat16 [9, 32], P('groups'), may hold values from -2 to 2
- mix_weight: bfloat16 [32, 32], P('groups'), may hold values from -1 to 1
- mix_bias: float32 [32], P('groups'), may hold values from -3 to 3
- proj_weight: bfloat16 [32, 6], P('groups'), may hold values from -1 to 1
- proj_bias: float32 [6], P('groups'), may hold values from -3 to 3
- spectral_weight: float32 [2, 512, 32, 1024], P('groups', 'px')
- first_moment: float32 [2, 512, 32, 1024], P('groups', 'px'), may hold values from -3 to 3
- second_moment: float32 [2, 512, 32, 1024], P('groups', 'px'), may hold values from 0.0001 to 0.03
Outputs:
- stress: bfloat16 [6, 64, 256, 256], P('groups', 'px')
- loss: float32 [1], P('groups')
- first_new: float32 [2, 512, 32, 1024], P('groups', 'px')
- step: float32 [2, 512, 32, 1024], P('groups', 'px')
The draws below stay inside these ranges and needn't reach their ends.
All inputs are finite; a program needn't handle non-finite values.
Results may differ from the reference program's by a relative error of at most 0.0028.
The reference program's roundings to bfloat16 on the way count: a program that leaves them out, or rounds other values in their place, can miss the bound.
Values sent between devices are 32-bit elements; how exact they have to be, the bound alone decides.
A program may use at most 192 MiB of HBM per device.

```python
import math
import jax
import jax.numpy as jnp
from jax import lax

CX = 2
NY = 256
NZ = 256
WIDTH = 32
MODES = 16
IN_CH = 9
OUT_CH = 6
NX = 64
PAIRS = 512
XMODES = 32


def draw_target(key, part):
    shape = (OUT_CH, NX, NY, NZ)
    across = jnp.arange(NX, dtype=jnp.float32) / max(NX - 1, 1)
    comps = jnp.arange(OUT_CH, dtype=jnp.float32) / max(OUT_CH - 1, 1)
    comp_scale = jnp.power(3.0, comps)[:, None, None, None]
    base = jnp.clip(jax.random.normal(key, shape, jnp.float32), -4.0, 4.0)
    amplitude = 0.5 * jnp.power(3.0, across)[None, :, None, None] * comp_scale
    return jnp.clip(base * amplitude, -34.0, 34.0).astype(jnp.bfloat16)


def draw_spectral_weight(key, part):
    shape = (2, 2 * MODES * MODES, 2 * MODES, WIDTH * WIDTH)
    sigma = 0.7 / math.sqrt(16.0 * MODES ** 3 * WIDTH / (NX * NY * NZ))
    values = jnp.clip(jax.random.normal(key, shape, jnp.float32), -5.0, 5.0)
    return values * sigma


def block_scale(rng, dims, split, smallest, high):
    factor_of = 1.0
    for dim, shards_of in split:
        draws = jax.random.uniform(jax.random.fold_in(jax.random.fold_in(rng, 6), dim), (shards_of,), jnp.float32, smallest / len(split), high / len(split))
        factor_of = factor_of * jnp.repeat(jnp.exp(draws), dims[dim] // shards_of).reshape((-1,) + (1,) * (len(dims) - 1 - dim))
    return factor_of


def normal_values(rng, shape, scale, reach, shards=(), kind=jnp.bfloat16):
    values = jax.random.normal(rng, shape, jnp.float32) * scale
    if len(shards) > 0:
        values = block_scale(rng, shape, shards, -0.22, 0.18) * values
    return jnp.clip(values, min=-reach, max=reach).astype(kind)


def setup_inputs(seed: int = 0, part: int = 0) -> dict:
    key_list = jax.random.split(jax.random.key(seed), 11)
    part_splits = jax.random.split(jax.random.fold_in(key_list[10], part), 11)
    fields = normal_values(part_splits[0], (IN_CH, NX, NY, NZ), 1.0, 6.0, ((1, 32),))
    target = draw_target(jax.random.fold_in(jax.random.fold_in(key_list[10], part), 71), part)
    lift_weight = normal_values(part_splits[2], (IN_CH, WIDTH), IN_CH ** -0.5, 2.0)
    mix_weight = normal_values(part_splits[3], (WIDTH, WIDTH), WIDTH ** -0.5, 1.0)
    mix_bias = normal_values(part_splits[4], (WIDTH,), 0.5, 3.0, (), jnp.float32)
    proj_weight = normal_values(part_splits[5], (WIDTH, OUT_CH), WIDTH ** -0.5, 1.0)
    proj_bias = normal_values(part_splits[6], (OUT_CH,), 0.5, 3.0, (), jnp.float32)
    spectral_weight = draw_spectral_weight(jax.random.fold_in(jax.random.fold_in(key_list[10], part), 71), part)
    first_moment = normal_values(part_splits[8], (2, PAIRS, XMODES, WIDTH * WIDTH), 0.2, 3.0, ((1, 32),), jnp.float32)
    second_moment = jnp.clip(jnp.exp(math.log(0.03) - 5.7037825 * jax.random.uniform(part_splits[9], (2, PAIRS, XMODES, WIDTH * WIDTH), jnp.float32) ** block_scale(part_splits[9], (2, PAIRS, XMODES, WIDTH * WIDTH), ((1, 32),), -0.2, 0.2)), 0.0001, 0.03)
    return {"fields": fields, "target": target, "lift_weight": lift_weight, "mix_weight": mix_weight, "mix_bias": mix_bias, "proj_weight": proj_weight, "proj_bias": proj_bias, "spectral_weight": spectral_weight, "first_moment": first_moment, "second_moment": second_moment}


highest = lax.Precision.HIGHEST
beta_first = 0.9
beta_second = 0.999
adam_eps = 1e-08
root_two = math.sqrt(2.0)
root_two_pi = math.sqrt(2.0 * math.pi)

def signed_modes(modes):
    index = jnp.arange(2 * modes, dtype=jnp.int32)
    return jnp.where(index < modes, index, index - 2 * modes)

def phase_table(freqs, points, length):
    product = jnp.remainder(freqs[:, None] * points[None, :], length)
    return product.astype(jnp.float32) * (2.0 * math.pi / length)

def pair_table(modes, points, length):
    angle = phase_table(signed_modes(modes), points, length)
    scale = 1.0 / math.sqrt(length)
    return (jnp.cos(angle) * scale, jnp.sin(angle) * scale)

def forward_z_table(modes, length):
    angle = phase_table(jnp.arange(modes, dtype=jnp.int32), jnp.arange(length, dtype=jnp.int32), length)
    scale = 1.0 / math.sqrt(length)
    return (jnp.concatenate([jnp.cos(angle), -jnp.sin(angle)], 0) * scale).astype(jnp.bfloat16)

def inverse_z_table(modes, length):
    angle = phase_table(jnp.arange(modes, dtype=jnp.int32), jnp.arange(length, dtype=jnp.int32), length)
    factor = jnp.where(jnp.arange(modes, dtype=jnp.int32) == 0, 1.0, 2.0).astype(jnp.float32)[:, None] / math.sqrt(length)
    return jnp.concatenate([jnp.cos(angle) * factor, -jnp.sin(angle) * factor], 0)

def lift_field(fields, lift_weight):
    lifted = jnp.einsum('ic,ixyz->cxyz', lift_weight.astype(jnp.float32), fields.astype(jnp.float32), precision=highest)
    return lifted.astype(jnp.bfloat16)

def forward_yz(field, z_fwd, y_both, modes):
    spec_z = jnp.einsum('qz,cxyz->qcxy', z_fwd.astype(jnp.float32), field.astype(jnp.float32), precision=highest)
    both = jnp.einsum('qcxy,py->cxqp', spec_z, y_both, precision=highest)
    half = 2 * modes
    real_part = both[:, :, :modes, :half] + both[:, :, modes:, half:]
    imag_part = both[:, :, modes:, :half] - both[:, :, :modes, half:]
    shape = real_part.shape
    flat = (shape[0], shape[1], shape[2] * shape[3])
    return jnp.stack([real_part.reshape(flat), imag_part.reshape(flat)], 0)

def forward_x(spectrum, x_both, modes):
    half = 2 * modes
    out = jnp.einsum('rcnl,qn->lrqc', spectrum, x_both, precision=highest)
    return (out[:, 0, :half] + out[:, 1, half:], out[:, 1, :half] - out[:, 0, half:])

def mix_modes(weight, in_real, in_imag):
    pairs, xmodes, chans = in_real.shape
    w_real = weight[0].reshape(pairs, xmodes, chans, chans)
    w_imag = weight[1].reshape(pairs, xmodes, chans, chans)

    def apply(matrix, vector):
        return jnp.einsum('lkco,lkc->lko', matrix, vector, precision=highest)
    return (apply(w_real, in_real) - apply(w_imag, in_imag), apply(w_real, in_imag) + apply(w_imag, in_real))

def inverse_x(out_real, out_imag, x_cos, x_sin):
    data = jnp.stack([out_real, out_imag], 0)
    tables = jnp.stack([x_cos, x_sin], 0)
    out = jnp.einsum('rlkc,tkn->rtcnl', data, tables, precision=highest)
    return jnp.stack([out[0, 0] - out[1, 1], out[1, 0] + out[0, 1]], 0)

def inverse_yz(grid, y_cos, y_sin, z_inv, modes):
    chans = grid.shape[1]
    planes = grid.shape[2]
    shaped = grid.reshape(2, chans, planes, modes, 2 * modes)
    tables = jnp.stack([y_cos, y_sin], 0)
    out = jnp.einsum('rcxzk,tky->rtzcxy', shaped, tables, precision=highest)
    stacked = jnp.concatenate([out[0, 0] - out[1, 1], out[1, 0] + out[0, 1]], 0)
    return jnp.einsum('qcxy,qz->cxyz', stacked, z_inv, precision=highest)

def pointwise(lifted, spatial, target, mix_weight, mix_bias, proj_weight, proj_bias):
    pre = jnp.einsum('co,cxyz->oxyz', mix_weight.astype(jnp.float32), lifted.astype(jnp.float32), precision=highest)
    pre = pre + mix_bias[:, None, None, None] + spatial
    cdf = 0.5 * (1.0 + lax.erf(pre / root_two))
    act = (pre * cdf).astype(jnp.bfloat16)
    pred = jnp.einsum('co,cxyz->oxyz', proj_weight.astype(jnp.float32), act.astype(jnp.float32), precision=highest)
    pred = pred + proj_bias[:, None, None, None]
    error = pred - target.astype(jnp.float32)
    error_sum = jnp.sum(error * error)
    error_b = error.astype(jnp.bfloat16)
    back = jnp.einsum('co,oxyz->cxyz', proj_weight.astype(jnp.float32), error_b.astype(jnp.float32), precision=highest)
    slope = cdf + pre * jnp.exp(-0.5 * pre * pre) / root_two_pi
    return (pred.astype(jnp.bfloat16), error_sum, (back * slope).astype(jnp.bfloat16))

def adam_direction(first_moment, second_moment, grad_real_out, grad_imag_out, in_real, in_imag):
    pairs, xmodes, chans = in_real.shape
    grad_real = in_real[:, :, :, None] * grad_real_out[:, :, None, :] + in_imag[:, :, :, None] * grad_imag_out[:, :, None, :]
    grad_imag = in_real[:, :, :, None] * grad_imag_out[:, :, None, :] - in_imag[:, :, :, None] * grad_real_out[:, :, None, :]
    grad = jnp.stack([grad_real.reshape(pairs, xmodes, chans * chans), grad_imag.reshape(pairs, xmodes, chans * chans)], 0)
    first_new = beta_first * first_moment + (1.0 - beta_first) * grad
    second_new = beta_second * second_moment + (1.0 - beta_second) * grad * grad
    first_corr = 1.0 - beta_first ** 2
    second_corr = 1.0 - beta_second ** 2
    step = first_new / first_corr / (jnp.sqrt(second_new / second_corr) + adam_eps)
    return (first_new, step)

def reference(fields, target, lift_weight, mix_weight, mix_bias, proj_weight, proj_bias, spectral_weight, first_moment, second_moment):
    z_fwd = forward_z_table(MODES, NZ)
    z_inv = inverse_z_table(MODES, NZ)
    y_cos, y_sin = pair_table(MODES, jnp.arange(NY, dtype=jnp.int32), NY)
    x_cos, x_sin = pair_table(MODES, jnp.arange(NX, dtype=jnp.int32), NX)
    y_both = jnp.concatenate([y_cos, y_sin], 0)
    x_both = jnp.concatenate([x_cos, x_sin], 0)
    blocks = NX // CX

    def lift_block(index):
        start = (index * CX).astype(jnp.int32)
        piece = lax.dynamic_slice_in_dim(fields, start, CX, 1)
        return lift_field(piece, lift_weight)

    def first_pass(index):
        return forward_yz(lift_block(index), z_fwd, y_both, MODES)
    spectra = lax.map(first_pass, jnp.arange(blocks, dtype=jnp.int32))
    spectra = jnp.moveaxis(spectra, 0, 2).reshape(2, WIDTH, NX, PAIRS)
    in_real, in_imag = forward_x(spectra, x_both, MODES)
    out_real, out_imag = mix_modes(spectral_weight, in_real, in_imag)
    planes_back = inverse_x(out_real, out_imag, x_cos, x_sin)

    def second_pass(index):
        start = (index * CX).astype(jnp.int32)
        lifted = lift_block(index)
        spatial = inverse_yz(lax.dynamic_slice_in_dim(planes_back, start, CX, 2), y_cos, y_sin, z_inv, MODES)
        piece_target = lax.dynamic_slice_in_dim(target, start, CX, 1)
        stress_block, error_sum, grad_pre = pointwise(lifted, spatial, piece_target, mix_weight, mix_bias, proj_weight, proj_bias)
        return (stress_block, error_sum, forward_yz(grad_pre, z_fwd, y_both, MODES))
    stress_blocks, error_sums, grad_spectra = lax.map(second_pass, jnp.arange(blocks, dtype=jnp.int32))
    stress = jnp.moveaxis(stress_blocks, 0, 1).reshape(OUT_CH, NX, NY, NZ)
    grad_spectra = jnp.moveaxis(grad_spectra, 0, 2).reshape(2, WIDTH, NX, PAIRS)
    grad_real, grad_imag = forward_x(grad_spectra, x_both, MODES)
    kz_index = jnp.arange(PAIRS, dtype=jnp.int32) // (2 * MODES)
    weight_kz = jnp.where(kz_index == 0, 1.0, 2.0).astype(jnp.float32)[:, None, None]
    first_new, step = adam_direction(first_moment, second_moment, grad_real * weight_kz, grad_imag * weight_kz, in_real, in_imag)
    loss = (jnp.sum(error_sums) / (2.0 * OUT_CH * NX * NY * NZ)).reshape(1)
    return (stress, loss, first_new, step)
```

```python
import functools
import math

import jax
import jax.numpy as jnp
import numpy as np
from jax import lax
from jax.experimental import pallas as pl
from jax.experimental.pallas import tpu as pltpu
from jax.sharding import PartitionSpec as P

beta_first = 0.9
beta_second = 0.999
adam_eps = 1e-08
bf16 = jnp.bfloat16
f32 = jnp.float32
vmem_limit = 60 * 1024 * 1024


def trig(freqs, points, length):
    angle = np.remainder(freqs[:, None] * points[None, :], length) * (2.0 * math.pi / length)
    return np.cos(angle), np.sin(angle)


def split_table(table):
    table = table.astype(np.float32)
    high = table.astype(bf16)
    low = (table - high.astype(np.float32)).astype(bf16)
    return np.stack([high, low], 0)


def signed(modes):
    index = np.arange(2 * modes)
    return np.where(index < modes, index, index - 2 * modes)


def make_tables(modes, grid_x, grid_y, grid_z):
    half = 2 * modes
    cz, sz = trig(np.arange(modes), np.arange(grid_z), grid_z)
    z_fwd = (np.concatenate([cz, -sz], 0) / math.sqrt(grid_z)).astype(np.float32).astype(bf16)
    factor = np.where(np.arange(modes) == 0, 1.0, 2.0)[:, None] / math.sqrt(grid_z)
    z_inv = split_table(np.concatenate([cz * factor, -sz * factor], 0))
    z_rep = np.concatenate([z_inv[0], z_inv[0], z_inv[1], np.zeros_like(z_inv[0])], 0)
    cy, sy = trig(signed(modes), np.arange(grid_y), grid_y)
    cy, sy = cy / math.sqrt(grid_y), sy / math.sqrt(grid_y)
    order = np.arange(half).reshape(half // 4, 4).T

    def rows(real, imag):
        return np.stack([real[order], imag[order]], 1).reshape(2 * half, -1)

    y_fwd = np.stack([split_table(rows(cy, -sy)), split_table(rows(sy, cy))], 0)
    y_inv = split_table(np.concatenate([rows(cy, -sy), rows(sy, cy)], 1))
    cx, sx = trig(signed(modes), np.arange(grid_x), grid_x)
    cx, sx = cx / math.sqrt(grid_x), sx / math.sqrt(grid_x)
    x_fwd = split_table(np.concatenate([cx, sx], 0))
    x_inv = split_table(
        np.concatenate(
            [np.concatenate([cx.T, -sx.T], 1), np.concatenate([sx.T, cx.T], 1)], 0
        )
    )
    return z_fwd, z_rep, y_fwd, y_inv, x_fwd, x_inv


def dot(a, b):
    return jnp.dot(a, b, preferred_element_type=f32)


def dot_nt(a, b):
    return lax.dot_general(a, b, (((1,), (1,)), ((), ())), preferred_element_type=f32)


def parts_of(x):
    high = x.astype(bf16)
    return high, (x - high.astype(f32)).astype(bf16)


def table_dot(table, data):
    high, low = parts_of(data)
    return dot(table[0], high) + (dot(table[1], high) + dot(table[0], low))


def forward_yz(field_ref, zs_ref, z_fwd_ref, y_fwd_ref, out_ref, plane, modes):
    chans = field_ref.shape[0]
    z_fwd = z_fwd_ref[...]

    for c in range(chans):
        zs_ref[:, c, :] = dot_nt(z_fwd, field_ref[c])
    total = None
    for part in range(2):
        data = zs_ref[pl.ds(part * modes, modes)].reshape(modes * chans, zs_ref.shape[2])
        high, low = parts_of(data)
        t_high, t_low = y_fwd_ref[part, 0], y_fwd_ref[part, 1]
        term = dot_nt(t_high, high) + (dot_nt(t_low, high) + dot_nt(t_high, low))
        total = term if total is None else total + term
    devices, _, slots, _ = out_ref.shape
    quads = slots // 2
    per = total.shape[0] // 4
    groups = per // 2
    for k in range(modes):
        piece = jnp.concatenate(
            [
                total[j * per : (j + 1) * per, k * chans : (k + 1) * chans]
                for j in range(4)
            ],
            1,
        )
        for r in range(2):
            for h in range(groups // quads):
                row = r * groups + h * quads
                out_ref[k * (groups // quads) + h, plane, r * quads : (r + 1) * quads, :] = piece[
                    row : row + quads
                ]


def lift_kernel(modes, fields_ref, lift_ref, z_fwd_ref, y_fwd_ref, out_ref, field_ref, zs_ref):
    plane = pl.program_id(0)
    grid_y, grid_z = fields_ref.shape[2:]
    chans = field_ref.shape[0]

    def step(i, carry):
        at = pl.ds(pl.multiple_of(i * 16, 16), 16)
        data = fields_ref[:, 0, at, :].reshape(-1, grid_z)
        lifted = dot(lift_ref[...], data).astype(bf16)
        field_ref[:, at, :] = lifted.reshape(chans, 16, grid_z)
        return carry

    lax.fori_loop(0, grid_y // 16, step, 0, unroll=2)
    forward_yz(field_ref, zs_ref, z_fwd_ref, y_fwd_ref, out_ref, plane, modes)


def forward_x(recv_ref, x_ref, quad):
    quads = recv_ref.shape[1] // 2
    half = x_ref.shape[1] // 2
    real = table_dot(x_ref, recv_ref[:, quad, :])
    imag = table_dot(x_ref, recv_ref[:, quads + quad, :])
    return real[:half] + imag[half:], imag[:half] - real[half:]


def lane_group(shape):
    return lax.broadcasted_iota(jnp.int32, shape, 1) // 32


def spread_rows(data):
    group = lane_group(data.shape)
    return jnp.concatenate([jnp.where(group == j, data, 0.0) for j in range(4)], 0)


def expand(data, e_ref):
    high, low = parts_of(spread_rows(data))
    return dot(high, e_ref[...]) + dot(low, e_ref[...])


def mix_kernel(recv_ref, weight_ref, x_fwd_ref, x_inv_ref, e_ref, vhat_ref, out_ref):
    quads = recv_ref.shape[1] // 2
    quad = pl.program_id(0)
    v_real, v_imag = forward_x(recv_ref, x_fwd_ref, quad)
    vhat_ref[0, 0], vhat_ref[0, 1] = v_real, v_imag
    a_real, a_imag = expand(v_real, e_ref), expand(v_imag, e_ref)
    half = v_real.shape[0]
    m_real, m_imag = None, None
    for t in range(8):
        lanes = slice(t * 128, (t + 1) * 128)
        w_real = weight_ref[0, :, :, lanes].reshape(4 * half, 128)
        w_imag = weight_ref[1, :, :, lanes].reshape(4 * half, 128)
        ar, ai = a_real[:, lanes], a_imag[:, lanes]
        pr = w_real * ar - w_imag * ai
        pi = w_real * ai + w_imag * ar
        m_real = pr if m_real is None else m_real + pr
        m_imag = pi if m_imag is None else m_imag + pi

    def gather(m):
        m = m + pltpu.roll(m, 64, 1)
        m = m + pltpu.roll(m, 32, 1)
        group = lane_group((half, 128))
        out = m[:half]
        for j in range(1, 4):
            out = jnp.where(group == j, m[j * half : (j + 1) * half], out)
        return out

    mixed = jnp.concatenate([gather(m_real), gather(m_imag)], 0)
    back = table_dot(x_inv_ref, mixed)
    grid_x = recv_ref.shape[0]
    out_ref[:, quad, :] = back[:grid_x]
    out_ref[:, quads + quad, :] = back[grid_x:]


poly = (0.254829592, -0.284496736, 1.421413741, -1.453152027, 1.061405429)
poly_p = 0.3275911


def gelu_parts(u):
    e = jnp.exp(u * u * -0.5)
    t = 1.0 / (1.0 + (poly_p / math.sqrt(2.0)) * jnp.abs(u))
    q = 0.5 * poly[4]
    for a in poly[3::-1]:
        q = q * t + 0.5 * a
    q = q * t * e
    cdf = jnp.where(u >= 0.0, 1.0 - q, q)
    return cdf, cdf + u * e * (1.0 / math.sqrt(2.0 * math.pi))


def plane_kernel(
    modes,
    recv_ref,
    fields_ref,
    target_ref,
    lift_ref,
    mix_ref,
    bias_ref,
    proj_ref,
    proj_t_ref,
    proj_bias_ref,
    z_fwd_ref,
    z_rep_ref,
    y_fwd_ref,
    y_inv_ref,
    stress_ref,
    out_ref,
    err_ref,
    field_ref,
    zs_ref,
    us_ref,
    v_ref,
):
    plane = pl.program_id(0)
    grid_y, grid_z = fields_ref.shape[2:]
    chans = field_ref.shape[0]
    comps = target_ref.shape[0]
    devices, _, slots, _ = recv_ref.shape
    quads = slots // 2
    per = 4 * modes // 4
    groups = per // 2
    halves = groups // quads
    columns = []
    for k in range(modes):
        g = jnp.concatenate(
            [
                recv_ref[k * halves + h, plane, r * quads : (r + 1) * quads, :]
                for r in range(2)
                for h in range(halves)
            ],
            0,
        )
        columns.append(
            jnp.concatenate([g[:, j * chans : (j + 1) * chans] for j in range(4)], 0)
        )
    spec = jnp.concatenate(columns, 1).T
    high, low = parts_of(spec)
    t_high, t_low = y_inv_ref[0], y_inv_ref[1]
    u = dot(high, t_high) + (dot(high, t_low) + dot(low, t_high))
    us_ref[...] = u.reshape(modes, chans, 2 * grid_y)
    for o in range(chans):
        row = us_ref[:, o, :]
        both = jnp.concatenate([row[:, :grid_y], row[:, grid_y:]], 0)
        b_high = both.astype(bf16).astype(f32)
        b_low = both - b_high
        stacked = jnp.concatenate([b_high, b_low, b_high, jnp.zeros_like(both)], 0)
        v_ref[o] = stacked.T.astype(bf16)

    def step(i, err):
        at = pl.ds(pl.multiple_of(i * 16, 16), 16)
        data = fields_ref[:, 0, at, :].reshape(-1, grid_z)
        lifted = dot(lift_ref[...], data).astype(bf16)
        spatial = dot(v_ref[:, at, :].reshape(chans * 16, -1), z_rep_ref[...])
        spatial = spatial.reshape(chans, 16, grid_z)
        target = target_ref[:, 0, at, :].astype(f32)
        stress, grads = [], []
        rows = chans * 8
        for h in range(2):
            pre = dot(mix_ref[...], lifted[h * rows : (h + 1) * rows])
            pre = pre.reshape(chans, 8, grid_z) + bias_ref[...]
            pre = pre + spatial[:, h * 8 : (h + 1) * 8]
            cdf, slope = gelu_parts(pre)
            act = (pre * cdf).astype(bf16).reshape(rows, grid_z)
            pred = dot(proj_ref[...], act).reshape(comps, 8, grid_z) + proj_bias_ref[...]
            stress.append(pred)
            error = pred - target[:, h * 8 : (h + 1) * 8]
            err = err + jnp.sum(error * error, 0)
            error_b = error.reshape(comps * 8, grid_z).astype(bf16)
            back = dot(proj_t_ref[...], error_b).reshape(chans, 8, grid_z)
            grads.append(back * slope)
        stress_ref[:, 0, at, :] = jnp.concatenate(stress, 1).astype(bf16)
        field_ref[:, at, :] = jnp.concatenate(grads, 1).astype(bf16)
        return err

    err = lax.fori_loop(0, grid_y // 16, step, jnp.zeros((8, grid_z), f32))
    folded = err[:, :128]
    for t in range(1, grid_z // 128):
        folded = folded + err[:, t * 128 : (t + 1) * 128]

    @pl.when(plane == 0)
    def _():
        err_ref[...] = folded

    @pl.when(plane > 0)
    def _():
        err_ref[...] += folded

    forward_yz(field_ref, zs_ref, z_fwd_ref, y_fwd_ref, out_ref, plane, modes)


def adam_kernel(
    recv_ref, vhat_ref, scale_ref, first_ref, second_ref, x_ref, e_ref, f_ref, first_out, step_out
):
    quad = pl.program_id(0)
    d_real, d_imag = forward_x(recv_ref, x_ref, quad)
    scale = scale_ref[0]
    b_real, b_imag = expand(d_real * scale, f_ref), expand(d_imag * scale, f_ref)
    a_real, a_imag = expand(vhat_ref[0, 0], e_ref), expand(vhat_ref[0, 1], e_ref)
    half = d_real.shape[0]
    first_corr = 1.0 / (1.0 - beta_first**2)
    second_corr = 1.0 / (1.0 - beta_second**2)
    for t in range(8):
        lanes = slice(t * 128, (t + 1) * 128)
        ar, ai = a_real[:, lanes], a_imag[:, lanes]
        grads = (ar * b_real + ai * b_imag, ar * b_imag - ai * b_real)
        for r in range(2):
            grad = grads[r].reshape(4, half, 128)
            first = beta_first * first_ref[r, :, :, lanes] + (1.0 - beta_first) * grad
            second = (
                beta_second * second_corr * second_ref[r, :, :, lanes]
                + ((1.0 - beta_second) * second_corr) * grad * grad
            )
            first_out[r, :, :, lanes] = first
            step_out[r, :, :, lanes] = first * first_corr / (jnp.sqrt(second) + adam_eps)


def exchange_kernel(axis, devices, count, *refs):
    sends, recvs = refs[:count], refs[count : 2 * count]
    send_sem, recv_sem, own_sem = refs[2 * count :]
    me = lax.axis_index(axis)
    barrier = pltpu.get_barrier_semaphore()

    def greet(off, carry):
        pl.semaphore_signal(
            barrier,
            inc=1,
            device_id={axis: lax.rem(me + off, devices)},
            device_id_type=pl.DeviceIdType.MESH,
        )
        return carry

    lax.fori_loop(1, devices, greet, 0)
    pl.semaphore_wait(barrier, devices - 1)

    def copy(i, off, there, slot):
        src = sends[i].at[there] if sends[i].shape == recvs[i].shape else sends[i]
        return pltpu.make_async_remote_copy(
            src_ref=src,
            dst_ref=recvs[i].at[slot],
            send_sem=send_sem.at[i, off],
            recv_sem=recv_sem.at[i, off],
            device_id={axis: there},
            device_id_type=pl.DeviceIdType.MESH,
        )

    def start(off, carry):
        for i in range(count):
            copy(i, off, lax.rem(me + off, devices), me).start()
        return carry

    def finish(off, carry):
        for i in range(count):
            copy(
                i, off, lax.rem(me + off, devices), lax.rem(me + devices - off, devices)
            ).wait()
        return carry

    lax.fori_loop(1, devices, start, 0)
    own = []
    for i in range(count):
        src = sends[i].at[me] if sends[i].shape == recvs[i].shape else sends[i]
        own.append(pltpu.make_async_copy(src, recvs[i].at[me], own_sem.at[i]))
        own[-1].start()
    for item in own:
        item.wait()
    lax.fori_loop(1, devices, finish, 0)


def exchange(arrays, devices, ident):
    count = len(arrays)
    shapes = [
        jax.ShapeDtypeStruct(a.shape if a.ndim == 4 else (devices,) + a.shape, a.dtype)
        for a in arrays
    ]
    return pl.pallas_call(
        functools.partial(exchange_kernel, "px", devices, count),
        out_shape=shapes,
        in_specs=[pl.BlockSpec(memory_space=pltpu.VMEM)] * count,
        out_specs=[pl.BlockSpec(memory_space=pltpu.VMEM)] * count,
        scratch_shapes=[
            pltpu.SemaphoreType.DMA((count, devices)),
            pltpu.SemaphoreType.DMA((count, devices)),
            pltpu.SemaphoreType.DMA((count,)),
        ],
        compiler_params=pltpu.CompilerParams(collective_id=ident, has_side_effects=True),
        name="exchange%d" % ident,
    )(*arrays)


def whole(shape):
    zeros = (0,) * len(shape)
    return pl.BlockSpec(tuple(shape), lambda i: zeros)


def spread(weight, size):
    eye = jnp.eye(size, dtype=weight.dtype)
    out = weight[:, None, :, None] * eye[None, :, None, :]
    return out.reshape(weight.shape[0] * size, weight.shape[1] * size)


def body(
    fields,
    target,
    lift_weight,
    mix_weight,
    mix_bias,
    proj_weight,
    proj_bias,
    spectral_weight,
    first_moment,
    second_moment,
):
    devices = lax.axis_size("px")
    rank = lax.axis_index("px")
    in_ch, planes, grid_y, grid_z = fields.shape
    chans = mix_weight.shape[0]
    comps = target.shape[0]
    half = spectral_weight.shape[2]
    modes = half // 2
    local_pairs = spectral_weight.shape[1]
    grid_x = planes * devices
    quads = local_pairs // 4
    slots = 2 * quads
    z_fwd, z_rep, y_fwd, y_inv, x_fwd, x_inv = (
        jnp.asarray(t) for t in make_tables(modes, grid_x, grid_y, grid_z)
    )
    lanes = np.arange(128) % 32
    e_table = jnp.asarray((lanes[:, None] == np.arange(1024)[None, :] // 32).astype(bf16))
    f_table = jnp.asarray((lanes[:, None] == lanes[None, :]).astype(bf16))
    chunk = (devices, planes, slots, 128)
    params = pltpu.CompilerParams(
        dimension_semantics=("arbitrary",), vmem_limit_bytes=vmem_limit
    )

    lift16 = spread(lift_weight.T, 16)
    lift_split = (
        lift16.reshape(chans, 2, 8, in_ch * 16).transpose(1, 0, 2, 3).reshape(chans * 16, -1)
    )
    mix8 = spread(mix_weight.T, 8)
    proj8 = spread(proj_weight.T, 8)
    proj8_t = spread(proj_weight, 8)

    plane_block = lambda n: pl.BlockSpec((n, 1, grid_y, grid_z), lambda p: (0, p, 0, 0))
    spectra = pl.pallas_call(
        functools.partial(lift_kernel, modes),
        grid=(planes,),
        out_shape=jax.ShapeDtypeStruct(chunk, f32),
        in_specs=[
            plane_block(in_ch),
            whole(lift16.shape),
            whole(z_fwd.shape),
            whole(y_fwd.shape),
        ],
        out_specs=whole(chunk),
        scratch_shapes=[
            pltpu.VMEM((chans, grid_y, grid_z), bf16),
            pltpu.VMEM((half, chans, grid_y), f32),
        ],
        compiler_params=params,
        name="lift_spectrum",
    )(fields, lift16, z_fwd, y_fwd)

    (moved,) = exchange([spectra], devices, 0)

    flat = (grid_x, slots, 128)
    pair_block = pl.BlockSpec((2, 4, half, 1024), lambda q: (0, q, 0, 0))
    vhat_block = pl.BlockSpec((1, 2, half, 128), lambda q: (q, 0, 0, 0))
    vhat, sending = pl.pallas_call(
        mix_kernel,
        grid=(quads,),
        out_shape=(
            jax.ShapeDtypeStruct((quads, 2, half, 128), f32),
            jax.ShapeDtypeStruct(flat, f32),
        ),
        in_specs=[
            whole(flat),
            pair_block,
            whole(x_fwd.shape),
            whole(x_inv.shape),
            whole(e_table.shape),
        ],
        out_specs=(vhat_block, whole(flat)),
        compiler_params=params,
        name="mix_modes",
    )(moved.reshape(flat), spectral_weight, x_fwd, x_inv, e_table)

    (result,) = exchange([sending.reshape(chunk)], devices, 1)

    bias = jnp.broadcast_to(mix_bias[:, None, None], (chans, 1, grid_z))
    pbias = jnp.broadcast_to(proj_bias[:, None, None], (comps, 1, grid_z))
    stress, grad_spectra, err = pl.pallas_call(
        functools.partial(plane_kernel, modes),
        grid=(planes,),
        out_shape=(
            jax.ShapeDtypeStruct(target.shape, bf16),
            jax.ShapeDtypeStruct(chunk, f32),
            jax.ShapeDtypeStruct((8, 128), f32),
        ),
        in_specs=[whole(chunk), plane_block(in_ch), plane_block(comps)]
        + [
            whole(a.shape)
            for a in (
                lift_split, mix8, bias, proj8, proj8_t, pbias, z_fwd, z_rep, y_fwd, y_inv
            )
        ],
        out_specs=(plane_block(comps), whole(chunk), whole((8, 128))),
        scratch_shapes=[
            pltpu.VMEM((chans, grid_y, grid_z), bf16),
            pltpu.VMEM((half, chans, grid_y), f32),
            pltpu.VMEM((modes, chans, 2 * grid_y), f32),
            pltpu.VMEM((chans, grid_y, 8 * modes), bf16),
        ],
        compiler_params=params,
        name="planes",
    )(
        result, fields, target, lift_split, mix8, bias, proj8, proj8_t, pbias,
        z_fwd, z_rep, y_fwd, y_inv,
    )

    grads_moved, errors = exchange([grad_spectra, err], devices, 2)
    loss = (jnp.sum(errors) / (2.0 * comps * grid_x * grid_y * grid_z)).reshape(1)

    kz_index = (rank * local_pairs + jnp.arange(local_pairs, dtype=jnp.int32)) // half
    scale = jnp.where(kz_index == 0, 1.0, 2.0).astype(f32)
    scale = jnp.repeat(scale, 32).reshape(quads, 1, 128)
    first_new, step = pl.pallas_call(
        adam_kernel,
        grid=(quads,),
        out_shape=(
            jax.ShapeDtypeStruct(first_moment.shape, f32),
            jax.ShapeDtypeStruct(first_moment.shape, f32),
        ),
        in_specs=[
            whole(flat),
            vhat_block,
            pl.BlockSpec((1, 1, 128), lambda q: (q, 0, 0)),
            pair_block,
            pair_block,
            whole(x_fwd.shape),
            whole(e_table.shape),
            whole(f_table.shape),
        ],
        out_specs=(pair_block, pair_block),
        compiler_params=params,
        name="adam",
    )(
        grads_moved.reshape(flat), vhat, scale, first_moment, second_moment,
        x_fwd, e_table, f_table,
    )
    return (stress, loss, first_new, step)


def solution(mesh):
    placed = (
        P("groups", "px", None, None),
        P("groups", "px", None, None),
        P("groups", None),
        P("groups", None),
        P("groups"),
        P("groups", None),
        P("groups"),
        P("groups", "px", None, None),
        P("groups", "px", None, None),
        P("groups", "px", None, None),
    )
    return jax.shard_map(
        body,
        mesh=mesh,
        in_specs=placed,
        out_specs=(
            P("groups", "px", None, None),
            P("groups"),
            P("groups", "px", None, None),
            P("groups", "px", None, None),
        ),
        check_vma=False,
    )
```

```python
import functools
import math

import jax
import jax.numpy as jnp
import numpy as np
from jax import lax
from jax.experimental import pallas as pl
from jax.experimental.pallas import tpu as pltpu
from jax.sharding import PartitionSpec as P

beta_first = 0.9
beta_second = 0.999
adam_eps = 1e-08
bf16 = jnp.bfloat16
f32 = jnp.float32
vmem_limit = 60 * 1024 * 1024


def trig(freqs, points, length):
    angle = np.remainder(freqs[:, None] * points[None, :], length) * (2.0 * math.pi / length)
    return np.cos(angle), np.sin(angle)


def split_table(table):
    table = table.astype(np.float32)
    high = table.astype(bf16)
    low = (table - high.astype(np.float32)).astype(bf16)
    return np.stack([high, low], 0)


def signed(modes):
    index = np.arange(2 * modes)
    return np.where(index < modes, index, index - 2 * modes)


def make_tables(modes, grid_x, grid_y, grid_z):
    half = 2 * modes
    cz, sz = trig(np.arange(modes), np.arange(grid_z), grid_z)
    z_fwd = (np.concatenate([cz, -sz], 0) / math.sqrt(grid_z)).astype(np.float32).astype(bf16)
    factor = np.where(np.arange(modes) == 0, 1.0, 2.0)[:, None] / math.sqrt(grid_z)
    z_inv = split_table(np.concatenate([cz * factor, -sz * factor], 0))
    z_rep = np.concatenate([z_inv[0], z_inv[0], z_inv[1], np.zeros_like(z_inv[0])], 0)
    cy, sy = trig(signed(modes), np.arange(grid_y), grid_y)
    cy, sy = cy / math.sqrt(grid_y), sy / math.sqrt(grid_y)
    order = np.arange(half).reshape(half // 4, 4).T

    def rows(real, imag):
        return np.stack([real[order], imag[order]], 1).reshape(2 * half, -1)

    y_fwd = np.stack([split_table(rows(cy, -sy)), split_table(rows(sy, cy))], 0)
    y_inv = split_table(np.concatenate([rows(cy, -sy), rows(sy, cy)], 1))
    cx, sx = trig(signed(modes), np.arange(grid_x), grid_x)
    cx, sx = cx / math.sqrt(grid_x), sx / math.sqrt(grid_x)
    x_fwd = split_table(np.concatenate([cx, sx], 0))
    x_inv = split_table(
        np.concatenate(
            [np.concatenate([cx.T, -sx.T], 1), np.concatenate([sx.T, cx.T], 1)], 0
        )
    )
    return z_fwd, z_rep, y_fwd, y_inv, x_fwd, x_inv


def dot(a, b):
    return jnp.dot(a, b, preferred_element_type=f32)


def dot_nt(a, b):
    return lax.dot_general(a, b, (((1,), (1,)), ((), ())), preferred_element_type=f32)


def parts_of(x):
    high = x.astype(bf16)
    return high, (x - high.astype(f32)).astype(bf16)


def table_dot(table, data):
    high, low = parts_of(data)
    t_high, t_low = table[0].astype(bf16), table[1].astype(bf16)
    return dot(t_high, high) + (dot(t_low, high) + dot(t_high, low))


def forward_yz(field_ref, zs_ref, z_fwd_ref, y_fwd_ref, out_ref, plane, modes):
    chans = field_ref.shape[0]
    z_fwd = z_fwd_ref[...].astype(bf16)

    for c in range(chans):
        zs_ref[:, c, :] = dot_nt(z_fwd, field_ref[c])
    total = None
    for part in range(2):
        data = zs_ref[pl.ds(part * modes, modes)].reshape(modes * chans, zs_ref.shape[2])
        high, low = parts_of(data)
        t_high, t_low = (y_fwd_ref[part, i].astype(bf16) for i in range(2))
        term = dot_nt(t_high, high) + (dot_nt(t_low, high) + dot_nt(t_high, low))
        total = term if total is None else total + term
    devices, _, slots, _ = out_ref.shape
    quads = slots // 2
    per = total.shape[0] // 4
    groups = per // 2
    for k in range(modes):
        piece = jnp.concatenate(
            [
                total[j * per : (j + 1) * per, k * chans : (k + 1) * chans]
                for j in range(4)
            ],
            1,
        )
        for r in range(2):
            for h in range(groups // quads):
                row = r * groups + h * quads
                out_ref[k * (groups // quads) + h, plane, r * quads : (r + 1) * quads, :] = piece[
                    row : row + quads
                ]


def spread(weight, table_refs, flip):
    rows_ref, cols_ref, mask_ref = table_refs
    rows, cols = rows_ref[...].astype(bf16), cols_ref[...].astype(bf16)
    tall = dot_nt(rows, weight) if flip else dot(rows, weight)
    return (dot(tall.astype(bf16), cols) * mask_ref[...]).astype(bf16)


def lift_kernel(
    modes,
    fields_ref,
    weight_ref,
    rows_ref,
    cols_ref,
    mask_ref,
    z_fwd_ref,
    y_fwd_ref,
    out_ref,
    field_ref,
    zs_ref,
    lift_ref,
):
    plane = pl.program_id(0)

    @pl.when(plane == 0)
    def _():
        lift_ref[...] = spread(weight_ref[...], (rows_ref, cols_ref, mask_ref), True)

    grid_y, grid_z = fields_ref.shape[2:]
    chans = field_ref.shape[0]

    def step(i, carry):
        at = pl.ds(pl.multiple_of(i * 16, 16), 16)
        data = fields_ref[:, 0, at, :].reshape(-1, grid_z)
        lifted = dot(lift_ref[...], data).astype(bf16)
        field_ref[:, at, :] = lifted.reshape(chans, 16, grid_z)
        return carry

    lax.fori_loop(0, grid_y // 16, step, 0, unroll=2)
    forward_yz(field_ref, zs_ref, z_fwd_ref, y_fwd_ref, out_ref, plane, modes)


def forward_x(recv_ref, x_ref, quad):
    quads = recv_ref.shape[1] // 2
    half = x_ref.shape[1] // 2
    real = table_dot(x_ref, recv_ref[:, quad, :])
    imag = table_dot(x_ref, recv_ref[:, quads + quad, :])
    return real[:half] + imag[half:], imag[:half] - real[half:]


def lane_group(shape):
    return lax.broadcasted_iota(jnp.int32, shape, 1) // 32


def spread_rows(data):
    group = lane_group(data.shape)
    return jnp.concatenate([jnp.where(group == j, data, 0.0) for j in range(4)], 0)


def expand(data, e_ref):
    high, low = parts_of(spread_rows(data))
    table = e_ref[...].astype(bf16)
    return dot(high, table) + dot(low, table)


def mix_kernel(recv_ref, weight_ref, x_fwd_ref, x_inv_ref, e_ref, vhat_ref, out_ref):
    quads = recv_ref.shape[1] // 2
    quad = pl.program_id(0)
    v_real, v_imag = forward_x(recv_ref, x_fwd_ref, quad)
    vhat_ref[0, 0], vhat_ref[0, 1] = v_real, v_imag
    a_real, a_imag = expand(v_real, e_ref), expand(v_imag, e_ref)
    half = v_real.shape[0]
    m_real, m_imag = None, None
    for t in range(8):
        lanes = slice(t * 128, (t + 1) * 128)
        w_real = weight_ref[0, :, :, lanes].reshape(4 * half, 128)
        w_imag = weight_ref[1, :, :, lanes].reshape(4 * half, 128)
        ar, ai = a_real[:, lanes], a_imag[:, lanes]
        pr = w_real * ar - w_imag * ai
        pi = w_real * ai + w_imag * ar
        m_real = pr if m_real is None else m_real + pr
        m_imag = pi if m_imag is None else m_imag + pi

    def gather(m):
        m = m + pltpu.roll(m, 64, 1)
        m = m + pltpu.roll(m, 32, 1)
        group = lane_group((half, 128))
        out = m[:half]
        for j in range(1, 4):
            out = jnp.where(group == j, m[j * half : (j + 1) * half], out)
        return out

    mixed = jnp.concatenate([gather(m_real), gather(m_imag)], 0)
    back = table_dot(x_inv_ref, mixed)
    grid_x = recv_ref.shape[0]
    out_ref[:, quad, :] = back[:grid_x]
    out_ref[:, quads + quad, :] = back[grid_x:]


poly = (0.254829592, -0.284496736, 1.421413741, -1.453152027, 1.061405429)
poly_p = 0.3275911


def gelu_parts(u):
    e = jnp.exp(u * u * -0.5)
    d = 1.0 + (poly_p / math.sqrt(2.0)) * jnp.abs(u)
    t = pl.reciprocal(d, approx=True)
    t = t * (2.0 - d * t)
    q = 0.5 * poly[4]
    for a in poly[3::-1]:
        q = q * t + 0.5 * a
    q = q * t * e
    cdf = jnp.where(u >= 0.0, 1.0 - q, q)
    return cdf, cdf + u * e * (1.0 / math.sqrt(2.0 * math.pi))


def plane_kernel(
    modes,
    recv_ref,
    fields_ref,
    target_ref,
    lift_weight_ref,
    mix_weight_ref,
    mix_bias_ref,
    proj_weight_ref,
    comp_bias_ref,
    lift_rows_ref,
    lift_cols_ref,
    lift_mask_ref,
    chan_rows_ref,
    chan_cols_ref,
    chan_mask_ref,
    comp_rows_ref,
    comp_cols_ref,
    down_mask_ref,
    up_mask_ref,
    z_fwd_ref,
    z_rep_ref,
    y_fwd_ref,
    y_inv_ref,
    stress_ref,
    out_ref,
    err_ref,
    field_ref,
    zs_ref,
    us_ref,
    v_ref,
    lift_ref,
    mix_ref,
    proj_ref,
    proj_t_ref,
    bias_ref,
    proj_bias_ref,
):
    plane = pl.program_id(0)

    @pl.when(plane == 0)
    def _():
        proj = proj_weight_ref[...]
        lift_ref[...] = spread(
            lift_weight_ref[...], (lift_rows_ref, lift_cols_ref, lift_mask_ref), True
        )
        mix_ref[...] = spread(
            mix_weight_ref[...], (chan_rows_ref, chan_cols_ref, chan_mask_ref), True
        )
        proj_ref[...] = spread(proj, (comp_rows_ref, chan_cols_ref, down_mask_ref), True)
        proj_t_ref[...] = spread(proj, (chan_rows_ref, comp_cols_ref, up_mask_ref), False)
        for c in range(bias_ref.shape[0]):
            bias_ref[c] = jnp.full(bias_ref.shape[1:], mix_bias_ref[c], f32)
        for c in range(proj_bias_ref.shape[0]):
            proj_bias_ref[c] = jnp.full(proj_bias_ref.shape[1:], comp_bias_ref[c], f32)

    grid_y, grid_z = fields_ref.shape[2:]
    chans = field_ref.shape[0]
    comps = target_ref.shape[0]
    devices, _, slots, _ = recv_ref.shape
    quads = slots // 2
    per = 4 * modes // 4
    groups = per // 2
    halves = groups // quads
    columns = []
    for k in range(modes):
        g = jnp.concatenate(
            [
                recv_ref[k * halves + h, plane, r * quads : (r + 1) * quads, :]
                for r in range(2)
                for h in range(halves)
            ],
            0,
        )
        columns.append(
            jnp.concatenate([g[:, j * chans : (j + 1) * chans] for j in range(4)], 0)
        )
    spec = jnp.concatenate(columns, 1).T
    high, low = parts_of(spec)
    t_high, t_low = (y_inv_ref[i].astype(bf16) for i in range(2))
    z_rep = z_rep_ref[...].astype(bf16)
    u = dot(high, t_high) + (dot(high, t_low) + dot(low, t_high))
    us_ref[...] = u.reshape(modes, chans, 2 * grid_y)
    for o in range(chans):
        row = us_ref[:, o, :]
        both = jnp.concatenate([row[:, :grid_y], row[:, grid_y:]], 0)
        b_high = both.astype(bf16).astype(f32)
        b_low = both - b_high
        stacked = jnp.concatenate([b_high, b_low, b_high, jnp.zeros_like(both)], 0)
        v_ref[o] = stacked.T.astype(bf16)

    def step(i, err):
        at = pl.ds(pl.multiple_of(i * 16, 16), 16)
        data = fields_ref[:, 0, at, :].reshape(-1, grid_z)
        lifted = dot(lift_ref[...], data).astype(bf16)
        spatial = dot(v_ref[:, at, :].reshape(chans * 16, -1), z_rep)
        spatial = spatial.reshape(chans, 16, grid_z)
        target = target_ref[:, 0, at, :].astype(f32)
        stress, grads = [], []
        rows = chans * 8
        for h in range(2):
            pre = dot(mix_ref[...], lifted[h * rows : (h + 1) * rows])
            pre = pre.reshape(chans, 8, grid_z) + bias_ref[...]
            pre = pre + spatial[:, h * 8 : (h + 1) * 8]
            cdf, slope = gelu_parts(pre)
            act = (pre * cdf).astype(bf16).reshape(rows, grid_z)
            pred = dot(proj_ref[...], act).reshape(comps, 8, grid_z) + proj_bias_ref[...]
            stress.append(pred)
            error = pred - target[:, h * 8 : (h + 1) * 8]
            err = err + jnp.sum(error * error, 0)
            error_b = error.reshape(comps * 8, grid_z).astype(bf16)
            back = dot(proj_t_ref[...], error_b).reshape(chans, 8, grid_z)
            grads.append(back * slope)
        stress_ref[:, 0, at, :] = jnp.concatenate(stress, 1).astype(bf16)
        field_ref[:, at, :] = jnp.concatenate(grads, 1).astype(bf16)
        return err

    err = lax.fori_loop(0, grid_y // 16, step, jnp.zeros((8, grid_z), f32))
    folded = err[:, :128]
    for t in range(1, grid_z // 128):
        folded = folded + err[:, t * 128 : (t + 1) * 128]

    @pl.when(plane == 0)
    def _():
        err_ref[...] = folded

    @pl.when(plane > 0)
    def _():
        err_ref[...] += folded

    forward_yz(field_ref, zs_ref, z_fwd_ref, y_fwd_ref, out_ref, plane, modes)


def adam_kernel(
    axis,
    cells,
    recv_ref,
    vhat_ref,
    errors_ref,
    first_ref,
    second_ref,
    x_ref,
    e_ref,
    f_ref,
    loss_out,
    first_out,
    step_out,
):
    quad = pl.program_id(0)

    @pl.when(quad == 0)
    def _():
        loss_out[0] = jnp.sum(jnp.sum(errors_ref[...], 0)) / cells

    d_real, d_imag = forward_x(recv_ref, x_ref, quad)
    pairs = 2 * recv_ref.shape[1]
    pair = lax.axis_index(axis) * pairs + quad * 4 + lane_group((1, 128))
    scale = jnp.where(pair < d_real.shape[0], 1.0, 2.0)
    b_real, b_imag = expand(d_real * scale, f_ref), expand(d_imag * scale, f_ref)
    a_real, a_imag = expand(vhat_ref[0, 0], e_ref), expand(vhat_ref[0, 1], e_ref)
    half = d_real.shape[0]
    first_corr = 1.0 / (1.0 - beta_first**2)
    second_corr = 1.0 / (1.0 - beta_second**2)
    for t in range(8):
        lanes = slice(t * 128, (t + 1) * 128)
        ar, ai = a_real[:, lanes], a_imag[:, lanes]
        grads = (ar * b_real + ai * b_imag, ar * b_imag - ai * b_real)
        for r in range(2):
            grad = grads[r].reshape(4, half, 128)
            first = beta_first * first_ref[r, :, :, lanes] + (1.0 - beta_first) * grad
            second = (
                beta_second * second_corr * second_ref[r, :, :, lanes]
                + ((1.0 - beta_second) * second_corr) * grad * grad
            )
            first_out[r, :, :, lanes] = first
            step_out[r, :, :, lanes] = first * first_corr / (jnp.sqrt(second) + adam_eps)


def exchange_kernel(axis, devices, count, *refs):
    sends, recvs = refs[:count], refs[count : 2 * count]
    send_sem, recv_sem, own_sem = refs[2 * count :]
    me = lax.axis_index(axis)
    barrier = pltpu.get_barrier_semaphore()

    def greet(off, carry):
        pl.semaphore_signal(
            barrier,
            inc=1,
            device_id={axis: lax.rem(me + off, devices)},
            device_id_type=pl.DeviceIdType.MESH,
        )
        return carry

    lax.fori_loop(1, devices, greet, 0)
    pl.semaphore_wait(barrier, devices - 1)

    def copy(i, off, there, slot):
        src = sends[i].at[there] if sends[i].shape == recvs[i].shape else sends[i]
        return pltpu.make_async_remote_copy(
            src_ref=src,
            dst_ref=recvs[i].at[slot],
            send_sem=send_sem.at[i, off],
            recv_sem=recv_sem.at[i, off],
            device_id={axis: there},
            device_id_type=pl.DeviceIdType.MESH,
        )

    def start(off, carry):
        for i in range(count):
            copy(i, off, lax.rem(me + off, devices), me).start()
        return carry

    def finish(off, carry):
        for i in range(count):
            copy(
                i, off, lax.rem(me + off, devices), lax.rem(me + devices - off, devices)
            ).wait()
        return carry

    lax.fori_loop(1, devices, start, 0)
    own = []
    for i in range(count):
        src = sends[i].at[me] if sends[i].shape == recvs[i].shape else sends[i]
        own.append(pltpu.make_async_copy(src, recvs[i].at[me], own_sem.at[i]))
        own[-1].start()
    for item in own:
        item.wait()
    lax.fori_loop(1, devices, finish, 0)


def exchange(arrays, devices, ident):
    count = len(arrays)
    shapes = [
        jax.ShapeDtypeStruct(a.shape if a.ndim == 4 else (devices,) + a.shape, a.dtype)
        for a in arrays
    ]
    return pl.pallas_call(
        functools.partial(exchange_kernel, "px", devices, count),
        out_shape=shapes,
        in_specs=[pl.BlockSpec(memory_space=pltpu.VMEM)] * count,
        out_specs=[pl.BlockSpec(memory_space=pltpu.VMEM)] * count,
        scratch_shapes=[
            pltpu.SemaphoreType.DMA((count, devices)),
            pltpu.SemaphoreType.DMA((count, devices)),
            pltpu.SemaphoreType.DMA((count,)),
        ],
        compiler_params=pltpu.CompilerParams(collective_id=ident, has_side_effects=True),
        name="exchange%d" % ident,
    )(*arrays)


def whole(shape):
    zeros = (0,) * len(shape)
    return pl.BlockSpec(tuple(shape), lambda i: zeros)


def spread_tables(rows, cols, size, halves=1):
    inner = size // halves
    row_y = np.tile(np.arange(inner), rows)
    row_y = np.concatenate([row_y + h * inner for h in range(halves)])
    row_of = np.tile(np.repeat(np.arange(rows), inner), halves)
    col_of, col_y = np.repeat(np.arange(cols), size), np.tile(np.arange(size), cols)
    return tuple(
        jnp.asarray(t.astype(np.float32))
        for t in (
            row_of[:, None] == np.arange(rows)[None, :],
            np.arange(cols)[:, None] == col_of[None, :],
            row_y[:, None] == col_y[None, :],
        )
    )


def body(
    fields,
    target,
    lift_weight,
    mix_weight,
    mix_bias,
    proj_weight,
    proj_bias,
    spectral_weight,
    first_moment,
    second_moment,
):
    devices = lax.axis_size("px")
    in_ch, planes, grid_y, grid_z = fields.shape
    chans = mix_weight.shape[0]
    comps = target.shape[0]
    half = spectral_weight.shape[2]
    modes = half // 2
    local_pairs = spectral_weight.shape[1]
    grid_x = planes * devices
    quads = local_pairs // 4
    slots = 2 * quads
    z_fwd, z_rep, y_fwd, y_inv, x_fwd, x_inv = (
        jnp.asarray(t.astype(np.float32)) for t in make_tables(modes, grid_x, grid_y, grid_z)
    )
    lanes = np.arange(128) % 32
    e_table = jnp.asarray((lanes[:, None] == np.arange(1024)[None, :] // 32).astype(np.float32))
    f_table = jnp.asarray((lanes[:, None] == lanes[None, :]).astype(np.float32))
    chunk = (devices, planes, slots, 128)
    params = pltpu.CompilerParams(
        dimension_semantics=("arbitrary",), vmem_limit_bytes=vmem_limit
    )

    lift_rows, lift_cols, lift_mask = spread_tables(chans, in_ch, 16)
    split_rows, split_cols, split_mask = spread_tables(chans, in_ch, 16, 2)
    chan_rows, chan_cols, chan_mask = spread_tables(chans, chans, 8)
    comp_rows, _, down_mask = spread_tables(comps, chans, 8)
    _, comp_cols, up_mask = spread_tables(chans, comps, 8)
    smem = pl.BlockSpec(memory_space=pltpu.SMEM)

    plane_block = lambda n: pl.BlockSpec((n, 1, grid_y, grid_z), lambda p: (0, p, 0, 0))
    spectra = pl.pallas_call(
        functools.partial(lift_kernel, modes),
        grid=(planes,),
        out_shape=jax.ShapeDtypeStruct(chunk, f32),
        in_specs=[
            plane_block(in_ch),
            whole(lift_weight.shape),
            whole(lift_rows.shape),
            whole(lift_cols.shape),
            whole(lift_mask.shape),
            whole(z_fwd.shape),
            whole(y_fwd.shape),
        ],
        out_specs=whole(chunk),
        scratch_shapes=[
            pltpu.VMEM((chans, grid_y, grid_z), bf16),
            pltpu.VMEM((half, chans, grid_y), f32),
            pltpu.VMEM(lift_mask.shape, bf16),
        ],
        compiler_params=params,
        name="lift_spectrum",
    )(fields, lift_weight, lift_rows, lift_cols, lift_mask, z_fwd, y_fwd)

    (moved,) = exchange([spectra], devices, 0)

    flat = (grid_x, slots, 128)
    pair_block = pl.BlockSpec((2, 4, half, 1024), lambda q: (0, q, 0, 0))
    vhat_block = pl.BlockSpec((1, 2, half, 128), lambda q: (q, 0, 0, 0))
    vhat, sending = pl.pallas_call(
        mix_kernel,
        grid=(quads,),
        out_shape=(
            jax.ShapeDtypeStruct((quads, 2, half, 128), f32),
            jax.ShapeDtypeStruct(flat, f32),
        ),
        in_specs=[
            whole(flat),
            pair_block,
            whole(x_fwd.shape),
            whole(x_inv.shape),
            whole(e_table.shape),
        ],
        out_specs=(vhat_block, whole(flat)),
        compiler_params=params,
        name="mix_modes",
    )(moved.reshape(flat), spectral_weight, x_fwd, x_inv, e_table)

    (result,) = exchange([sending.reshape(chunk)], devices, 1)

    tables = (
        split_rows, split_cols, split_mask, chan_rows, chan_cols, chan_mask,
        comp_rows, comp_cols, down_mask, up_mask, z_fwd, z_rep, y_fwd, y_inv,
    )
    stress, grad_spectra, err = pl.pallas_call(
        functools.partial(plane_kernel, modes),
        grid=(planes,),
        out_shape=(
            jax.ShapeDtypeStruct(target.shape, bf16),
            jax.ShapeDtypeStruct(chunk, f32),
            jax.ShapeDtypeStruct((8, 128), f32),
        ),
        in_specs=[whole(chunk), plane_block(in_ch), plane_block(comps)]
        + [whole(lift_weight.shape), whole(mix_weight.shape), smem]
        + [whole(proj_weight.shape), smem]
        + [whole(a.shape) for a in tables],
        out_specs=(plane_block(comps), whole(chunk), whole((8, 128))),
        scratch_shapes=[
            pltpu.VMEM((chans, grid_y, grid_z), bf16),
            pltpu.VMEM((half, chans, grid_y), f32),
            pltpu.VMEM((modes, chans, 2 * grid_y), f32),
            pltpu.VMEM((chans, grid_y, 8 * modes), bf16),
            pltpu.VMEM(split_mask.shape, bf16),
            pltpu.VMEM(chan_mask.shape, bf16),
            pltpu.VMEM(down_mask.shape, bf16),
            pltpu.VMEM(up_mask.shape, bf16),
            pltpu.VMEM((chans, 1, grid_z), f32),
            pltpu.VMEM((comps, 1, grid_z), f32),
        ],
        compiler_params=params,
        name="planes",
    )(
        result, fields, target, lift_weight, mix_weight, mix_bias, proj_weight, proj_bias,
        *tables,
    )

    grads_moved, errors = exchange([grad_spectra, err], devices, 2)
    cells = 2.0 * comps * grid_x * grid_y * grid_z
    loss, first_new, step = pl.pallas_call(
        functools.partial(adam_kernel, "px", cells),
        grid=(quads,),
        out_shape=(
            jax.ShapeDtypeStruct((1,), f32),
            jax.ShapeDtypeStruct(first_moment.shape, f32),
            jax.ShapeDtypeStruct(first_moment.shape, f32),
        ),
        in_specs=[
            whole(flat),
            vhat_block,
            whole(errors.shape),
            pair_block,
            pair_block,
            whole(x_fwd.shape),
            whole(e_table.shape),
            whole(f_table.shape),
        ],
        out_specs=(smem, pair_block, pair_block),
        compiler_params=params,
        name="adam",
    )(
        grads_moved.reshape(flat), vhat, errors, first_moment, second_moment,
        x_fwd, e_table, f_table,
    )
    return (stress, loss, first_new, step)


def solution(mesh):
    placed = (
        P("groups", "px", None, None),
        P("groups", "px", None, None),
        P("groups", None),
        P("groups", None),
        P("groups"),
        P("groups", None),
        P("groups"),
        P("groups", "px", None, None),
        P("groups", "px", None, None),
        P("groups", "px", None, None),
    )
    return jax.shard_map(
        body,
        mesh=mesh,
        in_specs=placed,
        out_specs=(
            P("groups", "px", None, None),
            P("groups"),
            P("groups", "px", None, None),
            P("groups", "px", None, None),
        ),
        check_vma=False,
    )
```

```python
import functools
import math

import jax
import jax.numpy as jnp
import numpy as np
from jax import lax
from jax.experimental import pallas as pl
from jax.experimental.pallas import tpu as pltpu
from jax.sharding import PartitionSpec as P

beta_first = 0.9
beta_second = 0.999
adam_eps = 1e-08
bf16 = jnp.bfloat16
f32 = jnp.float32
vmem_limit = 60 * 1024 * 1024


def trig(freqs, points, length):
    angle = np.remainder(freqs[:, None] * points[None, :], length) * (2.0 * math.pi / length)
    return np.cos(angle), np.sin(angle)


def split_table(table):
    table = table.astype(np.float32)
    high = table.astype(bf16)
    low = (table - high.astype(np.float32)).astype(bf16)
    return np.stack([high, low], 0)


def signed(modes):
    index = np.arange(2 * modes)
    return np.where(index < modes, index, index - 2 * modes)


def make_tables(modes, grid_x, grid_y, grid_z):
    half = 2 * modes
    cz, sz = trig(np.arange(modes), np.arange(grid_z), grid_z)
    z_fwd = (np.concatenate([cz, -sz], 0) / math.sqrt(grid_z)).astype(np.float32).astype(bf16)
    factor = np.where(np.arange(modes) == 0, 1.0, 2.0)[:, None] / math.sqrt(grid_z)
    z_inv = split_table(np.concatenate([cz * factor, -sz * factor], 0))
    z_rep = np.concatenate([z_inv[0], z_inv[0], z_inv[1], np.zeros_like(z_inv[0])], 0)
    cy, sy = trig(signed(modes), np.arange(grid_y), grid_y)
    cy, sy = cy / math.sqrt(grid_y), sy / math.sqrt(grid_y)
    order = np.arange(half).reshape(half // 4, 4).T

    def rows(real, imag):
        return np.stack([real[order], imag[order]], 1).reshape(2 * half, -1)

    y_fwd = np.stack([split_table(rows(cy, -sy)), split_table(rows(sy, cy))], 0)
    y_inv = split_table(np.concatenate([rows(cy, -sy), rows(sy, cy)], 1))
    cx, sx = trig(signed(modes), np.arange(grid_x), grid_x)
    cx, sx = cx / math.sqrt(grid_x), sx / math.sqrt(grid_x)
    x_fwd = split_table(np.concatenate([cx, sx], 0))
    x_inv = split_table(
        np.concatenate(
            [np.concatenate([cx.T, -sx.T], 1), np.concatenate([sx.T, cx.T], 1)], 0
        )
    )
    return z_fwd, z_rep, y_fwd, y_inv, x_fwd, x_inv


def dot(a, b):
    return jnp.dot(a, b, preferred_element_type=f32)


def dot_nt(a, b):
    return lax.dot_general(a, b, (((1,), (1,)), ((), ())), preferred_element_type=f32)


def parts_of(x):
    high = x.astype(bf16)
    return high, (x - high.astype(f32)).astype(bf16)


def table_dot(table, data):
    high, low = parts_of(data)
    t_high, t_low = table[0].astype(bf16), table[1].astype(bf16)
    return dot(t_high, high) + (dot(t_low, high) + dot(t_high, low))


def forward_yz(field_ref, zs_ref, z_fwd_ref, y_fwd_ref, out_ref, plane, modes):
    chans = field_ref.shape[0]
    z_fwd = z_fwd_ref[...].astype(bf16)

    for c in range(chans):
        zs_ref[:, c, :] = dot_nt(z_fwd, field_ref[c])
    total = None
    for part in range(2):
        data = zs_ref[pl.ds(part * modes, modes)].reshape(modes * chans, zs_ref.shape[2])
        high, low = parts_of(data)
        t_high, t_low = (y_fwd_ref[part, i].astype(bf16) for i in range(2))
        term = dot_nt(t_high, high) + (dot_nt(t_low, high) + dot_nt(t_high, low))
        total = term if total is None else total + term
    devices, _, slots, _ = out_ref.shape
    quads = slots // 2
    per = total.shape[0] // 4
    groups = per // 2
    for k in range(modes):
        piece = jnp.concatenate(
            [
                total[j * per : (j + 1) * per, k * chans : (k + 1) * chans]
                for j in range(4)
            ],
            1,
        )
        for r in range(2):
            for h in range(groups // quads):
                row = r * groups + h * quads
                out_ref[k * (groups // quads) + h, plane, r * quads : (r + 1) * quads, :] = piece[
                    row : row + quads
                ]


def spread(weight, table_refs, flip):
    rows_ref, cols_ref, mask_ref = table_refs
    rows, cols = rows_ref[...].astype(bf16), cols_ref[...].astype(bf16)
    tall = dot_nt(rows, weight) if flip else dot(rows, weight)
    return (dot(tall.astype(bf16), cols) * mask_ref[...]).astype(bf16)


def lift_kernel(
    modes,
    fields_ref,
    weight_ref,
    rows_ref,
    cols_ref,
    mask_ref,
    z_fwd_ref,
    y_fwd_ref,
    out_ref,
    field_ref,
    zs_ref,
    lift_ref,
):
    plane = pl.program_id(0)

    @pl.when(plane == 0)
    def _():
        lift_ref[...] = spread(weight_ref[...], (rows_ref, cols_ref, mask_ref), True)

    grid_y, grid_z = fields_ref.shape[2:]
    chans = field_ref.shape[0]

    def step(i, carry):
        at = pl.ds(pl.multiple_of(i * 16, 16), 16)
        data = fields_ref[:, 0, at, :].reshape(-1, grid_z)
        lifted = dot(lift_ref[...], data).astype(bf16)
        field_ref[:, at, :] = lifted.reshape(chans, 16, grid_z)
        return carry

    lax.fori_loop(0, grid_y // 16, step, 0, unroll=2)
    forward_yz(field_ref, zs_ref, z_fwd_ref, y_fwd_ref, out_ref, plane, modes)


def forward_x(recv_ref, x_ref, quad):
    quads = recv_ref.shape[1] // 2
    half = x_ref.shape[1] // 2
    real = table_dot(x_ref, recv_ref[:, quad, :])
    imag = table_dot(x_ref, recv_ref[:, quads + quad, :])
    return real[:half] + imag[half:], imag[:half] - real[half:]


def lane_group(shape):
    return lax.broadcasted_iota(jnp.int32, shape, 1) // 32


def spread_rows(data):
    group = lane_group(data.shape)
    return jnp.concatenate([jnp.where(group == j, data, 0.0) for j in range(4)], 0)


def expand(data, e_ref):
    high, low = parts_of(spread_rows(data))
    table = e_ref[...].astype(bf16)
    return dot(high, table) + dot(low, table)


def mix_kernel(recv_ref, weight_ref, x_fwd_ref, x_inv_ref, e_ref, vhat_ref, out_ref):
    quads = recv_ref.shape[1] // 2
    quad = pl.program_id(0)
    v_real, v_imag = forward_x(recv_ref, x_fwd_ref, quad)
    vhat_ref[0, 0], vhat_ref[0, 1] = v_real, v_imag
    a_real, a_imag = expand(v_real, e_ref), expand(v_imag, e_ref)
    half = v_real.shape[0]
    m_real, m_imag = None, None
    for t in range(8):
        lanes = slice(t * 128, (t + 1) * 128)
        w_real = weight_ref[0, :, :, lanes].reshape(4 * half, 128)
        w_imag = weight_ref[1, :, :, lanes].reshape(4 * half, 128)
        ar, ai = a_real[:, lanes], a_imag[:, lanes]
        pr = w_real * ar - w_imag * ai
        pi = w_real * ai + w_imag * ar
        m_real = pr if m_real is None else m_real + pr
        m_imag = pi if m_imag is None else m_imag + pi

    def gather(m):
        m = m + pltpu.roll(m, 64, 1)
        m = m + pltpu.roll(m, 32, 1)
        group = lane_group((half, 128))
        out = m[:half]
        for j in range(1, 4):
            out = jnp.where(group == j, m[j * half : (j + 1) * half], out)
        return out

    mixed = jnp.concatenate([gather(m_real), gather(m_imag)], 0)
    back = table_dot(x_inv_ref, mixed)
    grid_x = recv_ref.shape[0]
    out_ref[:, quad, :] = back[:grid_x]
    out_ref[:, quads + quad, :] = back[grid_x:]


poly = (0.254829592, -0.284496736, 1.421413741, -1.453152027, 1.061405429)
poly_p = 0.3275911


def gelu_parts(u):
    e = jnp.exp(u * u * -0.5)
    d = 1.0 + (poly_p / math.sqrt(2.0)) * jnp.abs(u)
    t = pl.reciprocal(d, approx=True)
    t = t * (2.0 - d * t)
    q = 0.5 * poly[4]
    for a in poly[3::-1]:
        q = q * t + 0.5 * a
    q = q * t * e
    cdf = jnp.where(u >= 0.0, 1.0 - q, q)
    return cdf, cdf + u * e * (1.0 / math.sqrt(2.0 * math.pi))


def plane_kernel(
    modes,
    recv_ref,
    fields_ref,
    target_ref,
    lift_weight_ref,
    mix_weight_ref,
    mix_bias_ref,
    proj_weight_ref,
    comp_bias_ref,
    lift_rows_ref,
    lift_cols_ref,
    lift_mask_ref,
    chan_rows_ref,
    chan_cols_ref,
    chan_mask_ref,
    comp_rows_ref,
    comp_cols_ref,
    down_mask_ref,
    up_mask_ref,
    z_fwd_ref,
    z_rep_ref,
    y_fwd_ref,
    y_inv_ref,
    stress_ref,
    out_ref,
    err_ref,
    field_ref,
    zs_ref,
    us_ref,
    v_ref,
    lift_ref,
    mix_ref,
    proj_ref,
    proj_t_ref,
    bias_ref,
    proj_bias_ref,
):
    plane = pl.program_id(0)

    @pl.when(plane == 0)
    def _():
        proj = proj_weight_ref[...]
        lift_ref[...] = spread(
            lift_weight_ref[...], (lift_rows_ref, lift_cols_ref, lift_mask_ref), True
        )
        mix_ref[...] = spread(
            mix_weight_ref[...], (chan_rows_ref, chan_cols_ref, chan_mask_ref), True
        )
        proj_ref[...] = spread(proj, (comp_rows_ref, chan_cols_ref, down_mask_ref), True)
        proj_t_ref[...] = spread(proj, (chan_rows_ref, comp_cols_ref, up_mask_ref), False)
        for c in range(bias_ref.shape[0]):
            bias_ref[c] = jnp.full(bias_ref.shape[1:], mix_bias_ref[c], f32)
        for c in range(proj_bias_ref.shape[0]):
            proj_bias_ref[c] = jnp.full(proj_bias_ref.shape[1:], comp_bias_ref[c], f32)

    grid_y, grid_z = fields_ref.shape[2:]
    chans = field_ref.shape[0]
    comps = target_ref.shape[0]
    devices, _, slots, _ = recv_ref.shape
    quads = slots // 2
    per = 4 * modes // 4
    groups = per // 2
    halves = groups // quads
    columns = []
    for k in range(modes):
        g = jnp.concatenate(
            [
                recv_ref[k * halves + h, plane, r * quads : (r + 1) * quads, :]
                for r in range(2)
                for h in range(halves)
            ],
            0,
        )
        columns.append(
            jnp.concatenate([g[:, j * chans : (j + 1) * chans] for j in range(4)], 0)
        )
    spec = jnp.concatenate(columns, 1).T
    high, low = parts_of(spec)
    t_high, t_low = (y_inv_ref[i].astype(bf16) for i in range(2))
    z_rep = z_rep_ref[...].astype(bf16)
    u = dot(high, t_high) + (dot(high, t_low) + dot(low, t_high))
    us_ref[...] = u.reshape(modes, chans, 2 * grid_y)
    for o in range(chans):
        row = us_ref[:, o, :]
        both = jnp.concatenate([row[:, :grid_y], row[:, grid_y:]], 0)
        b_high = both.astype(bf16).astype(f32)
        b_low = both - b_high
        stacked = jnp.concatenate([b_high, b_low, b_high, jnp.zeros_like(both)], 0)
        v_ref[o] = stacked.T.astype(bf16)

    def step(i, err):
        at = pl.ds(pl.multiple_of(i * 16, 16), 16)
        data = fields_ref[:, 0, at, :].reshape(-1, grid_z)
        lifted = dot(lift_ref[...], data).astype(bf16)
        spatial = dot(v_ref[:, at, :].reshape(chans * 16, -1), z_rep)
        spatial = spatial.reshape(chans, 16, grid_z)
        target = target_ref[:, 0, at, :].astype(f32)
        stress, grads = [], []
        rows = chans * 8
        for h in range(2):
            pre = dot(mix_ref[...], lifted[h * rows : (h + 1) * rows])
            pre = pre.reshape(chans, 8, grid_z) + bias_ref[...]
            pre = pre + spatial[:, h * 8 : (h + 1) * 8]
            cdf, slope = gelu_parts(pre)
            act = (pre * cdf).astype(bf16).reshape(rows, grid_z)
            pred = dot(proj_ref[...], act).reshape(comps, 8, grid_z) + proj_bias_ref[...]
            stress.append(pred)
            error = pred - target[:, h * 8 : (h + 1) * 8]
            err = err + jnp.sum(error * error, 0)
            error_b = error.reshape(comps * 8, grid_z).astype(bf16)
            back = dot(proj_t_ref[...], error_b).reshape(chans, 8, grid_z)
            grads.append(back * slope)
        stress_ref[:, 0, at, :] = jnp.concatenate(stress, 1).astype(bf16)
        field_ref[:, at, :] = jnp.concatenate(grads, 1).astype(bf16)
        return err

    err = lax.fori_loop(0, grid_y // 16, step, jnp.zeros((8, grid_z), f32), unroll=2)
    folded = err[:, :128]
    for t in range(1, grid_z // 128):
        folded = folded + err[:, t * 128 : (t + 1) * 128]

    @pl.when(plane == 0)
    def _():
        err_ref[...] = folded

    @pl.when(plane > 0)
    def _():
        err_ref[...] += folded

    forward_yz(field_ref, zs_ref, z_fwd_ref, y_fwd_ref, out_ref, plane, modes)


def adam_kernel(
    axis,
    cells,
    recv_ref,
    vhat_ref,
    errors_ref,
    first_ref,
    second_ref,
    x_ref,
    e_ref,
    f_ref,
    loss_out,
    first_out,
    step_out,
):
    quad = pl.program_id(0)

    @pl.when(quad == 0)
    def _():
        loss_out[0] = jnp.sum(jnp.sum(errors_ref[...], 0)) / cells

    d_real, d_imag = forward_x(recv_ref, x_ref, quad)
    pairs = 2 * recv_ref.shape[1]
    pair = lax.axis_index(axis) * pairs + quad * 4 + lane_group((1, 128))
    scale = jnp.where(pair < d_real.shape[0], 1.0, 2.0)
    b_real, b_imag = expand(d_real * scale, f_ref), expand(d_imag * scale, f_ref)
    a_real, a_imag = expand(vhat_ref[0, 0], e_ref), expand(vhat_ref[0, 1], e_ref)
    half = d_real.shape[0]
    first_corr = 1.0 / (1.0 - beta_first**2)
    second_corr = 1.0 / (1.0 - beta_second**2)
    for t in range(8):
        lanes = slice(t * 128, (t + 1) * 128)
        ar, ai = a_real[:, lanes], a_imag[:, lanes]
        grads = (ar * b_real + ai * b_imag, ar * b_imag - ai * b_real)
        for r in range(2):
            grad = grads[r].reshape(4, half, 128)
            first = beta_first * first_ref[r, :, :, lanes] + (1.0 - beta_first) * grad
            second = (
                beta_second * second_corr * second_ref[r, :, :, lanes]
                + ((1.0 - beta_second) * second_corr) * grad * grad
            )
            first_out[r, :, :, lanes] = first
            step_out[r, :, :, lanes] = first * first_corr / (jnp.sqrt(second) + adam_eps)


def exchange_kernel(axis, devices, count, *refs):
    sends, recvs = refs[:count], refs[count : 2 * count]
    send_sem, recv_sem, own_sem = refs[2 * count :]
    me = lax.axis_index(axis)
    barrier = pltpu.get_barrier_semaphore()

    def greet(off, carry):
        pl.semaphore_signal(
            barrier,
            inc=1,
            device_id={axis: lax.rem(me + off, devices)},
            device_id_type=pl.DeviceIdType.MESH,
        )
        return carry

    lax.fori_loop(1, devices, greet, 0)
    pl.semaphore_wait(barrier, devices - 1)

    def copy(i, off, there, slot):
        src = sends[i].at[there] if sends[i].shape == recvs[i].shape else sends[i]
        return pltpu.make_async_remote_copy(
            src_ref=src,
            dst_ref=recvs[i].at[slot],
            send_sem=send_sem.at[i, off],
            recv_sem=recv_sem.at[i, off],
            device_id={axis: there},
            device_id_type=pl.DeviceIdType.MESH,
        )

    def start(off, carry):
        for i in range(count):
            copy(i, off, lax.rem(me + off, devices), me).start()
        return carry

    def finish(off, carry):
        for i in range(count):
            copy(
                i, off, lax.rem(me + off, devices), lax.rem(me + devices - off, devices)
            ).wait()
        return carry

    lax.fori_loop(1, devices, start, 0)
    own = []
    for i in range(count):
        src = sends[i].at[me] if sends[i].shape == recvs[i].shape else sends[i]
        own.append(pltpu.make_async_copy(src, recvs[i].at[me], own_sem.at[i]))
        own[-1].start()
    for item in own:
        item.wait()
    lax.fori_loop(1, devices, finish, 0)


def exchange(arrays, devices, ident):
    count = len(arrays)
    shapes = [
        jax.ShapeDtypeStruct(a.shape if a.ndim == 4 else (devices,) + a.shape, a.dtype)
        for a in arrays
    ]
    return pl.pallas_call(
        functools.partial(exchange_kernel, "px", devices, count),
        out_shape=shapes,
        in_specs=[pl.BlockSpec(memory_space=pltpu.VMEM)] * count,
        out_specs=[pl.BlockSpec(memory_space=pltpu.VMEM)] * count,
        scratch_shapes=[
            pltpu.SemaphoreType.DMA((count, devices)),
            pltpu.SemaphoreType.DMA((count, devices)),
            pltpu.SemaphoreType.DMA((count,)),
        ],
        compiler_params=pltpu.CompilerParams(collective_id=ident, has_side_effects=True),
        name="exchange%d" % ident,
    )(*arrays)


def whole(shape):
    zeros = (0,) * len(shape)
    return pl.BlockSpec(tuple(shape), lambda i: zeros)


def spread_tables(rows, cols, size, halves=1):
    inner = size // halves
    row_y = np.tile(np.arange(inner), rows)
    row_y = np.concatenate([row_y + h * inner for h in range(halves)])
    row_of = np.tile(np.repeat(np.arange(rows), inner), halves)
    col_of, col_y = np.repeat(np.arange(cols), size), np.tile(np.arange(size), cols)
    return tuple(
        jnp.asarray(t.astype(np.float32))
        for t in (
            row_of[:, None] == np.arange(rows)[None, :],
            np.arange(cols)[:, None] == col_of[None, :],
            row_y[:, None] == col_y[None, :],
        )
    )


def body(
    fields,
    target,
    lift_weight,
    mix_weight,
    mix_bias,
    proj_weight,
    proj_bias,
    spectral_weight,
    first_moment,
    second_moment,
):
    devices = lax.axis_size("px")
    in_ch, planes, grid_y, grid_z = fields.shape
    chans = mix_weight.shape[0]
    comps = target.shape[0]
    half = spectral_weight.shape[2]
    modes = half // 2
    local_pairs = spectral_weight.shape[1]
    grid_x = planes * devices
    quads = local_pairs // 4
    slots = 2 * quads
    z_fwd, z_rep, y_fwd, y_inv, x_fwd, x_inv = (
        jnp.asarray(t.astype(np.float32)) for t in make_tables(modes, grid_x, grid_y, grid_z)
    )
    lanes = np.arange(128) % 32
    e_table = jnp.asarray((lanes[:, None] == np.arange(1024)[None, :] // 32).astype(np.float32))
    f_table = jnp.asarray((lanes[:, None] == lanes[None, :]).astype(np.float32))
    chunk = (devices, planes, slots, 128)
    params = pltpu.CompilerParams(
        dimension_semantics=("arbitrary",), vmem_limit_bytes=vmem_limit
    )

    lift_rows, lift_cols, lift_mask = spread_tables(chans, in_ch, 16)
    split_rows, split_cols, split_mask = spread_tables(chans, in_ch, 16, 2)
    chan_rows, chan_cols, chan_mask = spread_tables(chans, chans, 8)
    comp_rows, _, down_mask = spread_tables(comps, chans, 8)
    _, comp_cols, up_mask = spread_tables(chans, comps, 8)
    smem = pl.BlockSpec(memory_space=pltpu.SMEM)

    plane_block = lambda n: pl.BlockSpec((n, 1, grid_y, grid_z), lambda p: (0, p, 0, 0))
    spectra = pl.pallas_call(
        functools.partial(lift_kernel, modes),
        grid=(planes,),
        out_shape=jax.ShapeDtypeStruct(chunk, f32),
        in_specs=[
            plane_block(in_ch),
            whole(lift_weight.shape),
            whole(lift_rows.shape),
            whole(lift_cols.shape),
            whole(lift_mask.shape),
            whole(z_fwd.shape),
            whole(y_fwd.shape),
        ],
        out_specs=whole(chunk),
        scratch_shapes=[
            pltpu.VMEM((chans, grid_y, grid_z), bf16),
            pltpu.VMEM((half, chans, grid_y), f32),
            pltpu.VMEM(lift_mask.shape, bf16),
        ],
        compiler_params=params,
        name="lift_spectrum",
    )(fields, lift_weight, lift_rows, lift_cols, lift_mask, z_fwd, y_fwd)

    (moved,) = exchange([spectra], devices, 0)

    flat = (grid_x, slots, 128)
    pair_block = pl.BlockSpec((2, 4, half, 1024), lambda q: (0, q, 0, 0))
    vhat_block = pl.BlockSpec((1, 2, half, 128), lambda q: (q, 0, 0, 0))
    vhat, sending = pl.pallas_call(
        mix_kernel,
        grid=(quads,),
        out_shape=(
            jax.ShapeDtypeStruct((quads, 2, half, 128), f32),
            jax.ShapeDtypeStruct(flat, f32),
        ),
        in_specs=[
            whole(flat),
            pair_block,
            whole(x_fwd.shape),
            whole(x_inv.shape),
            whole(e_table.shape),
        ],
        out_specs=(vhat_block, whole(flat)),
        compiler_params=params,
        name="mix_modes",
    )(moved.reshape(flat), spectral_weight, x_fwd, x_inv, e_table)

    (result,) = exchange([sending.reshape(chunk)], devices, 1)

    tables = (
        split_rows, split_cols, split_mask, chan_rows, chan_cols, chan_mask,
        comp_rows, comp_cols, down_mask, up_mask, z_fwd, z_rep, y_fwd, y_inv,
    )
    stress, grad_spectra, err = pl.pallas_call(
        functools.partial(plane_kernel, modes),
        grid=(planes,),
        out_shape=(
            jax.ShapeDtypeStruct(target.shape, bf16),
            jax.ShapeDtypeStruct(chunk, f32),
            jax.ShapeDtypeStruct((8, 128), f32),
        ),
        in_specs=[whole(chunk), plane_block(in_ch), plane_block(comps)]
        + [whole(lift_weight.shape), whole(mix_weight.shape), smem]
        + [whole(proj_weight.shape), smem]
        + [whole(a.shape) for a in tables],
        out_specs=(plane_block(comps), whole(chunk), whole((8, 128))),
        scratch_shapes=[
            pltpu.VMEM((chans, grid_y, grid_z), bf16),
            pltpu.VMEM((half, chans, grid_y), f32),
            pltpu.VMEM((modes, chans, 2 * grid_y), f32),
            pltpu.VMEM((chans, grid_y, 8 * modes), bf16),
            pltpu.VMEM(split_mask.shape, bf16),
            pltpu.VMEM(chan_mask.shape, bf16),
            pltpu.VMEM(down_mask.shape, bf16),
            pltpu.VMEM(up_mask.shape, bf16),
            pltpu.VMEM((chans, 1, grid_z), f32),
            pltpu.VMEM((comps, 1, grid_z), f32),
        ],
        compiler_params=params,
        name="planes",
    )(
        result, fields, target, lift_weight, mix_weight, mix_bias, proj_weight, proj_bias,
        *tables,
    )

    grads_moved, errors = exchange([grad_spectra, err], devices, 2)
    cells = 2.0 * comps * grid_x * grid_y * grid_z
    loss, first_new, step = pl.pallas_call(
        functools.partial(adam_kernel, "px", cells),
        grid=(quads,),
        out_shape=(
            jax.ShapeDtypeStruct((1,), f32),
            jax.ShapeDtypeStruct(first_moment.shape, f32),
            jax.ShapeDtypeStruct(first_moment.shape, f32),
        ),
        in_specs=[
            whole(flat),
            vhat_block,
            whole(errors.shape),
            pair_block,
            pair_block,
            whole(x_fwd.shape),
            whole(e_table.shape),
            whole(f_table.shape),
        ],
        out_specs=(smem, pair_block, pair_block),
        compiler_params=params,
        name="adam",
    )(
        grads_moved.reshape(flat), vhat, errors, first_moment, second_moment,
        x_fwd, e_table, f_table,
    )
    return (stress, loss, first_new, step)


def solution(mesh):
    placed = (
        P("groups", "px", None, None),
        P("groups", "px", None, None),
        P("groups", None),
        P("groups", None),
        P("groups"),
        P("groups", None),
        P("groups"),
        P("groups", "px", None, None),
        P("groups", "px", None, None),
        P("groups", "px", None, None),
    )
    return jax.shard_map(
        body,
        mesh=mesh,
        in_specs=placed,
        out_specs=(
            P("groups", "px", None, None),
            P("groups"),
            P("groups", "px", None, None),
            P("groups", "px", None, None),
        ),
        check_vma=False,
    )
```
